32 devices in a mesh: groups: 2 (over y), rows: 4 (over z), tm: 2 (over x), cols: 2 (over core).
Axes of the slice: x: 2, y: 2, z: 4, core: 2. Of those that a mesh axis runs over, the one named last changes fastest.
Arguments:
- latents: bfloat16 [20, 4, 80, 384], P(('groups', 'tm'), 'rows', 'cols'), parts along dimension 0, may hold values from -16 to 16
- gain_one: float32 [384], replicated, may hold values from 0.1 to 1.9
- conv_one: bfloat16 [27, 384, 384], P(None, 'rows'), may hold values from -0.0625 to 0.0625
- bias_one: float32 [384], replicated, may hold values from -3 to 3
- gain_two: float32 [384], replicated, may hold values from 0.1 to 1.9
- conv_two: bfloat16 [27, 384, 384], P(None, 'rows'), may hold values from -0.0625 to 0.0625
- bias_two: float32 [384], replicated, may hold values from -3 to 3
Outputs:
- block_out: bfloat16 [20, 4, 80, 384], P(('groups', 'tm'), 'rows', 'cols'), parts along dimension 0
The draws below stay inside these ranges and needn't reach their ends.
There are 2 independent parts, one for each index of `groups`. The reference program is written for one: setup_inputs(seed, part) draws one part's arguments, and reference() takes and returns one part's arrays. A program takes and returns all parts, laid end to end along the dimension named above; an argument that names none is the same for every part. Nothing has to cross between parts.
All inputs are finite; a program needn't handle non-finite values.
Results may differ from the reference program's by a relative error of at most 0.006.
Values may be sent and summed in bfloat16 or wider, within the bound.
A program may use at most 64 MiB of HBM per device.

```python
import math
import jax
import jax.numpy as jnp
from jax import lax

C = 384
FRAMES = 10
HEIGHT = 4
WIDTH = 80


def draw_latents(key, part):
    first_key = jax.random.fold_in(key, 11)
    second_key = jax.random.fold_in(key, 12)
    normal_part = jnp.clip(jax.random.normal(first_key, (FRAMES, HEIGHT, WIDTH, C), jnp.float32), -5.0, 5.0)
    channel_scale = jnp.exp(jax.random.uniform(second_key, (C,), jnp.float32, math.log(0.3), math.log(3.0)))
    values = normal_part * channel_scale
    return jnp.clip(values, -16.0, 16.0).astype(jnp.bfloat16)


def block_scale(stream_key, shape, pieces, least, largest):
    level, own = 1.0, jax.random.fold_in(stream_key, 6)
    for dim, parts in pieces:
        draws = jnp.exp(jax.random.uniform(jax.random.fold_in(own, dim), (parts,), jnp.float32, least / len(pieces), largest / len(pieces)))
        level = level * jnp.repeat(draws, shape[dim] // parts).reshape([-1 if axis == dim else 1 for axis in range(len(shape))])
    return level


def gaussian(rng, shape, scale, limit, shards=(), kind=jnp.bfloat16):
    drawn = jax.random.normal(rng, shape, jnp.float32) * scale
    if len(shards) > 0:
        drawn = block_scale(rng, shape, shards, -0.22, 0.18) * drawn
    return jnp.clip(drawn, min=-limit, max=limit).astype(kind)


def setup_inputs(seed: int = 0, part: int = 0) -> dict:
    seeds = jax.random.split(jax.random.key(seed), 8)
    part_splits = jax.random.split(jax.random.fold_in(seeds[7], part), 8)
    return {
        "latents": draw_latents(jax.random.fold_in(jax.random.fold_in(seeds[7], part), 71), part),
        "gain_one": jnp.clip(1.0 + 0.18 * jax.random.normal(seeds[1], (C,), jnp.float32), 0.1, 1.9),
        "conv_one": gaussian(seeds[2], (27, C, C), (27 * C) ** -0.5, 0.0625, ((1, 4),)),
        "bias_one": gaussian(seeds[3], (C,), 0.5, 3.0, (), jnp.float32),
        "gain_two": jnp.clip(1.0 + 0.18 * jax.random.normal(seeds[4], (C,), jnp.float32), 0.1, 1.9),
        "conv_two": gaussian(seeds[5], (27, C, C), (27 * C) ** -0.5, 0.0625, ((1, 4),)),
        "bias_two": gaussian(seeds[6], (C,), 0.5, 3.0, (), jnp.float32),
    }


def activate(values, gain_values):
    values = values.astype(jnp.float32)
    mean_square = lax.optimization_barrier(jnp.mean(values * values, axis=-1, keepdims=True))
    return jax.nn.silu(values * lax.rsqrt(mean_square + 1e-06) * gain_values).astype(jnp.bfloat16)

def convolve(inputs, weight, bias_values):
    frames, height, breadth, channels = inputs.shape
    padded = jnp.pad(inputs, ((2, 0), (1, 1), (1, 1), (0, 0)))
    summed = jnp.zeros((frames * height * breadth, weight.shape[1]), jnp.float32)
    for depth_tap in range(3):
        for row_tap in range(3):
            for col_tap in range(3):
                window = padded[depth_tap:depth_tap + frames, row_tap:row_tap + height, col_tap:col_tap + breadth]
                window = window.reshape(frames * height * breadth, channels)
                kernel = weight[9 * depth_tap + 3 * row_tap + col_tap]
                summed = summed + lax.dot_general(window, kernel, (((1,), (1,)), ((), ())), preferred_element_type=jnp.float32)
    return summed.reshape(frames, height, breadth, weight.shape[1]) + bias_values

def reference(latents, gain_one, conv_one, bias_one, gain_two, conv_two, bias_two):
    first_act = activate(latents, gain_one)
    first_out = convolve(first_act, conv_one, bias_one).astype(jnp.bfloat16)
    second_act = activate(first_out, gain_two)
    branch = convolve(second_act, conv_two, bias_two)
    return (latents.astype(jnp.float32) + branch).astype(jnp.bfloat16)
```

```python
import functools

import jax
import jax.numpy as jnp
from jax import lax
from jax.experimental import pallas as pl
from jax.experimental.pallas import tpu as pltpu
from jax.sharding import PartitionSpec as P

MESH = pl.DeviceIdType.MESH
EPS = 1e-06


def up(value, multiple):
    return -(-value // multiple) * multiple


def activate(values, gain_values):
    mean_square = jnp.mean(values * values, axis=-1, keepdims=True)
    return jax.nn.silu(values * lax.rsqrt(mean_square + EPS) * gain_values)


def kernel(
    n_rows, n_tm, n_out,
    x_ref, g1_ref, w1_ref, b1_ref, g2_ref, w2_ref, b2_ref, out_ref,
    abuf, wbuf, zbuf, obuf, osend, psend, orecv, precv, edge_out, edge_in,
    w_sem, a_send, a_recv, e_send, e_recv, o_send, o_recv, p_send, p_recv,
):
    frames, _, width, chans = x_ref.shape
    cells = frames * width
    block = abuf.shape[2]
    head = block - 16
    lanes = wbuf.shape[3]
    r = lax.axis_index("rows")
    t = lax.axis_index("tm")
    c = lax.axis_index("cols")
    weights = (w1_ref, w2_ref)
    gains = (g1_ref, g2_ref)
    biases = (b1_ref, b2_ref)
    has_next = t + 1 < n_tm
    has_prev = t > 0
    distances = sorted(range(1, n_rows), key=lambda d: min(d, n_rows - d))

    def weight_copy(v, row_tap):
        return pltpu.make_async_copy(
            weights[v].at[:, row_tap],
            wbuf.at[v, :, :, pl.ds(0, weights[v].shape[3]), pl.ds(row_tap * chans, chans)],
            w_sem.at[v, row_tap],
        )

    for v in range(2):
        for row_tap in range(3):
            weight_copy(v, row_tap).start()

    barrier = pltpu.get_barrier_semaphore()

    def greet(where):
        pl.semaphore_signal(barrier, inc=1, device_id=where, device_id_type=MESH)

    for d in distances:
        greet({"rows": lax.rem(r + d, n_rows)})
    greet({"cols": 1 - c})

    @pl.when(has_next)
    def _():
        for j in range(n_rows):
            greet({"rows": j, "tm": t + 1})

    @pl.when(has_prev)
    def _():
        for j in range(n_rows):
            greet({"rows": j, "tm": t - 1})

    filled = weights[0].shape[3]
    for v in range(2):
        abuf[v, 0] = jnp.zeros((block, chans), jnp.bfloat16)
        abuf[v, n_rows + 1] = jnp.zeros((block, chans), jnp.bfloat16)
        if filled < lanes:
            wbuf[v, :, :, filled:, :] = jnp.zeros((3, 3, lanes - filled, 3 * chans), jnp.bfloat16)

    @pl.when(t == 0)
    def _():
        precv[...] = jnp.zeros(precv.shape, precv.dtype)

    def edge_copy(v):
        return pltpu.make_async_remote_copy(
            src_ref=edge_out.at[v], dst_ref=edge_in.at[v],
            send_sem=e_send.at[v], recv_sem=e_recv.at[v],
            device_id={"cols": 1 - c}, device_id_type=MESH,
        )

    def span(piece):
        return pl.ds(0, head) if piece == 0 else pl.ds(head, 16)

    def act_send(v, piece, d):
        part = abuf.at[v, r + 1, span(piece)]
        return pltpu.make_async_remote_copy(
            src_ref=part, dst_ref=part,
            send_sem=a_send.at[v, piece, d], recv_sem=a_recv.at[v, piece, r],
            device_id={"rows": lax.rem(r + d, n_rows)}, device_id_type=MESH,
        )

    def act_arrival(v, piece, j):
        part = abuf.at[v, j + 1, span(piece)]
        return pltpu.make_async_remote_copy(
            src_ref=part, dst_ref=part,
            send_sem=a_send.at[v, piece, 0], recv_sem=a_recv.at[v, piece, j],
            device_id={"rows": j}, device_id_type=MESH,
        )

    def out_copy(v, h, source):
        return pltpu.make_async_remote_copy(
            src_ref=osend.at[v, h], dst_ref=orecv.at[v, source],
            send_sem=o_send.at[v, h], recv_sem=o_recv.at[v, source],
            device_id={"rows": h}, device_id_type=MESH,
        )

    def past_copy(v, h, source):
        return pltpu.make_async_remote_copy(
            src_ref=psend.at[v, h], dst_ref=precv.at[v, source],
            send_sem=p_send.at[v, h], recv_sem=p_recv.at[v, source],
            device_id={"rows": h, "tm": t + 1}, device_id_type=MESH,
        )

    def spread(v, act):
        cube = act.reshape(frames, width, chans)
        edge = jnp.where(c == 0, cube[:, width - 1, :], cube[:, 0, :])
        edge = jnp.concatenate([edge, jnp.zeros((16 - frames, chans), jnp.float32)], axis=0)
        edge_out[v] = edge.astype(jnp.bfloat16)
        if v == 0:
            pl.semaphore_wait(
                barrier,
                n_rows + jnp.where(has_next, n_rows, 0) + jnp.where(has_prev, n_rows, 0),
            )
        edge_copy(v).start()
        abuf[v, r + 1, 0:head] = act[0:head].astype(jnp.bfloat16)
        for d in distances:
            act_send(v, 0, d).start()
        edge_copy(v).wait_recv()
        got = edge_in[v].astype(jnp.float32)
        last = jnp.concatenate([act[head:cells], got[0 : block - cells]], axis=0)
        abuf[v, r + 1, head:block] = last.astype(jnp.bfloat16)
        for d in distances:
            act_send(v, 1, d).start()

    def convolve(v):
        bias = jnp.zeros((1, n_out), jnp.float32)
        for j in range(n_rows):
            bias = bias + jnp.where(r == j, biases[v][:, j * n_out : (j + 1) * n_out], 0.0)
        if n_out < lanes:
            bias = jnp.concatenate([bias, jnp.zeros((1, lanes - n_out), jnp.float32)], axis=1)
        column = lax.broadcasted_iota(jnp.int32, (width, lanes), 0)
        edge_column = jnp.where(c == 0, width - 1, 0)
        for row_tap in range(3):
            weight_copy(v, row_tap).wait()

        def step(k, carry):
            h = lax.rem(r + k, n_rows)
            for off in (-1, 0, 1):
                j = h + off
                first = n_rows
                for e in (-1, 0, 1):
                    user = j + e
                    turn = lax.rem(user - r + 2 * n_rows, n_rows)
                    valid = (user >= 0) & (user < n_rows)
                    first = jnp.minimum(first, jnp.where(valid, turn, n_rows))

                @pl.when((j >= 0) & (j < n_rows) & (j != r) & (first == k))
                def _():
                    act_arrival(v, 0, j).wait_recv()
                    act_arrival(v, 1, j).wait_recv()

            window = jnp.concatenate([abuf[v, h], abuf[v, h + 1], abuf[v, h + 2]], axis=1)
            kernel_all = wbuf[v].reshape(9 * lanes, 3 * chans)
            zbuf[...] = lax.dot_general(
                window, kernel_all, (((1,), (1,)), ((), ())), preferred_element_type=jnp.float32
            )

            def piece(f, tap, s):
                at = (3 * tap + s) * lanes
                return zbuf[f * width : (f + 1) * width, at : at + lanes]

            sides = []
            for tap in range(3):
                left = zbuf[cells : cells + 8, 3 * tap * lanes : (3 * tap + 1) * lanes]
                right = zbuf[cells : cells + 8, (3 * tap + 2) * lanes : (3 * tap + 3) * lanes]
                sides.append(jnp.where(c == 0, right, left))
            for g in range(frames + 2):
                taps = [tap for tap in range(3) if 0 <= g - 2 + tap < frames]
                left, mid, right = (
                    functools.reduce(jnp.add, [piece(g - 2 + tap, tap, s) for tap in taps]) for s in range(3)
                )
                side = functools.reduce(
                    jnp.add, [sides[tap][g - 2 + tap : g - 1 + tap, :] for tap in taps]
                )
                total = mid + jnp.where(column > 0, pltpu.roll(left, 1, 0), 0.0)
                total = total + jnp.where(column < width - 1, pltpu.roll(right, width - 1, 0), 0.0)
                total = total + jnp.where(column == edge_column, side, 0.0)
                if g < frames:
                    total = total + bias
                obuf[g * width : (g + 1) * width, :] = total
            main = obuf[0:block, :].astype(jnp.bfloat16)

            @pl.when(k == 0)
            def _():
                orecv[v, r] = main

            @pl.when(k > 0)
            def _():
                osend[v, h] = main
                out_copy(v, h, r).start()

            @pl.when(has_next)
            def _():
                psend[v, h] = obuf[cells : cells + 2 * width, :].astype(jnp.bfloat16)
                past_copy(v, h, r).start()

            return carry

        lax.fori_loop(0, n_rows, step, 0)
        for d in distances:
            j = lax.rem(r + d, n_rows)
            out_copy(v, j, j).wait_recv()

        @pl.when(has_prev)
        def _():
            for j in range(n_rows):
                past_copy(v, j, j).wait_recv()

        parts = []
        for j in range(n_rows):
            main = orecv[v, j].astype(jnp.float32)
            past = precv[v, j].astype(jnp.float32)
            part = jnp.concatenate([main[0 : 2 * width] + past, main[2 * width : cells]], axis=0)
            parts.append(part[:, 0:n_out])
        return jnp.concatenate(parts, axis=1)

    latents = x_ref[...].astype(jnp.float32).reshape(cells, chans)
    spread(0, activate(latents, gains[0][...]))
    first_out = convolve(0).astype(jnp.bfloat16).astype(jnp.float32)
    spread(1, activate(first_out, gains[1][...]))
    branch = convolve(1)
    latents = x_ref[...].astype(jnp.float32).reshape(cells, chans)
    out_ref[...] = (latents + branch).reshape(frames, 1, width, chans).astype(jnp.bfloat16)

    for v in range(2):
        edge_copy(v).wait_send()
        for d in distances:
            act_send(v, 0, d).wait_send()
            act_send(v, 1, d).wait_send()
            out_copy(v, lax.rem(r + d, n_rows), r).wait_send()

    @pl.when(has_next)
    def _():
        for v in range(2):
            for j in range(n_rows):
                past_copy(v, j, r).wait_send()


def solution(mesh):
    n_rows = mesh.shape["rows"]
    n_tm = mesh.shape["tm"]

    def shards(latents, gain_one, conv_one, bias_one, gain_two, conv_two, bias_two):
        frames, _, width, chans = latents.shape
        n_out = conv_one.shape[1]
        lanes = up(n_out, 128)
        block = up(frames * width + frames, 16)

        def taps(weight):
            weight = weight.reshape(3, 3, 3, n_out, chans)
            extra = up(n_out, 16) - n_out
            if extra:
                weight = jnp.pad(weight, ((0, 0), (0, 0), (0, 0), (0, extra), (0, 0)))
            return weight

        vmem = pl.BlockSpec(memory_space=pltpu.VMEM)
        hbm = pl.BlockSpec(memory_space=pl.ANY)
        dma = pltpu.SemaphoreType.DMA
        bf16 = jnp.bfloat16
        flops = 2 * 2 * n_rows * frames * width * 27 * chans * n_out
        return pl.pallas_call(
            functools.partial(kernel, n_rows, n_tm, n_out),
            out_shape=jax.ShapeDtypeStruct(latents.shape, bf16),
            in_specs=[vmem, vmem, hbm, vmem, vmem, hbm, vmem],
            out_specs=vmem,
            scratch_shapes=[
                pltpu.VMEM((2, n_rows + 2, block, chans), bf16),
                pltpu.VMEM((2, 3, 3, lanes, 3 * chans), bf16),
                pltpu.VMEM((block, 9 * lanes), jnp.float32),
                pltpu.VMEM((up((frames + 2) * width, 16), lanes), jnp.float32),
                pltpu.VMEM((2, n_rows, block, lanes), bf16),
                pltpu.VMEM((2, n_rows, 2 * width, lanes), bf16),
                pltpu.VMEM((2, n_rows, block, lanes), bf16),
                pltpu.VMEM((2, n_rows, 2 * width, lanes), bf16),
                pltpu.VMEM((2, 16, chans), bf16),
                pltpu.VMEM((2, 16, chans), bf16),
                dma((2, 3)),
                dma((2, 2, n_rows)),
                dma((2, 2, n_rows)),
                dma((2,)),
                dma((2,)),
                dma((2, n_rows)),
                dma((2, n_rows)),
                dma((2, n_rows)),
                dma((2, n_rows)),
            ],
            compiler_params=pltpu.CompilerParams(
                collective_id=0, has_side_effects=True, vmem_limit_bytes=48 * 1024 * 1024
            ),
            cost_estimate=pl.CostEstimate(flops=flops, bytes_accessed=8 * 1024 * 1024, transcendentals=0),
        )(
            latents,
            gain_one.reshape(1, chans),
            taps(conv_one),
            bias_one.reshape(1, chans),
            gain_two.reshape(1, chans),
            taps(conv_two),
            bias_two.reshape(1, chans),
        )

    return jax.shard_map(
        shards,
        mesh=mesh,
        in_specs=(
            P(("groups", "tm"), "rows", "cols", None),
            P(),
            P(None, "rows", None),
            P(),
            P(),
            P(None, "rows", None),
            P(),
        ),
        out_specs=P(("groups", "tm"), "rows", "cols", None),
        check_vma=False,
    )
```

```python
import functools

import jax
import jax.numpy as jnp
from jax import lax
from jax.experimental import pallas as pl
from jax.experimental.pallas import tpu as pltpu
from jax.sharding import PartitionSpec as P

MESH = pl.DeviceIdType.MESH
EPS = 1e-06


def up(value, multiple):
    return -(-value // multiple) * multiple


def activate(values, gain_values):
    mean_square = jnp.mean(values * values, axis=-1, keepdims=True)
    return jax.nn.silu(values * lax.rsqrt(mean_square + EPS) * gain_values)


def kernel(
    n_rows, n_tm, n_out, tail,
    x_hbm, g1_ref, w1_ref, b1_ref, g2_ref, w2_ref, b2_ref, out_ref, x_ref,
    abuf, bbuf, wbuf, zbuf, obuf, fbuf, osend, orecv, psend, precv,
    edge_out, edge_in, edges_out, edges_in,
    x_sem, w_sem, a_send, a_recv, e_send, e_recv, es_send, es_recv,
    f_send, f_recv, o_send, o_recv, p_send, p_recv,
):
    frames, _, width, chans = x_ref.shape
    cells = frames * width
    block = abuf.shape[1]
    head = block - 16
    lanes = wbuf.shape[3]
    packed = fbuf.shape[2]
    keep = cells - tail
    spare = lanes - n_out
    r = lax.axis_index("rows")
    t = lax.axis_index("tm")
    c = lax.axis_index("cols")
    weights = (w1_ref, w2_ref)
    biases = (b1_ref, b2_ref)
    acts = (abuf, bbuf)
    has_next = t + 1 < n_tm
    has_prev = t > 0
    distances = sorted(range(1, n_rows), key=lambda d: min(d, n_rows - d))

    def peer(d):
        return lax.rem(r + d, n_rows)

    def weight_copy(v, row_tap):
        return pltpu.make_async_copy(
            weights[v].at[:, row_tap],
            wbuf.at[v, :, :, pl.ds(0, weights[v].shape[3]), pl.ds(row_tap * chans, chans)],
            w_sem.at[v, row_tap],
        )

    def remote(src, dst, send, recv, where):
        return pltpu.make_async_remote_copy(
            src_ref=src, dst_ref=dst, send_sem=send, recv_sem=recv, device_id=where, device_id_type=MESH
        )

    fetch = pltpu.make_async_copy(x_hbm, x_ref, x_sem)
    fetch.start()
    for v in range(2):
        for row_tap in range(3):
            weight_copy(v, row_tap).start()

    barrier = pltpu.get_barrier_semaphore()

    def greet(where):
        pl.semaphore_signal(barrier, inc=1, device_id=where, device_id_type=MESH)

    for d in distances:
        greet({"rows": peer(d)})
    greet({"cols": 1 - c})

    @pl.when(has_next)
    def _():
        greet({"tm": t + 1})

    @pl.when(has_prev)
    def _():
        greet({"tm": t - 1})

    filled = weights[0].shape[3]
    for v in range(2):
        acts[v][0] = jnp.zeros((block, chans), jnp.bfloat16)
        acts[v][n_rows + 1] = jnp.zeros((block, chans), jnp.bfloat16)
        if filled < lanes:
            wbuf[v, :, :, filled:, :] = jnp.zeros((3, 3, lanes - filled, 3 * chans), jnp.bfloat16)

    @pl.when(t == 0)
    def _():
        precv[...] = jnp.zeros(precv.shape, precv.dtype)

    def edge_copy():
        return remote(edge_out, edge_in, e_send, e_recv, {"cols": 1 - c})

    def edges_copy(h):
        return remote(edges_out.at[h], edges_in.at[h], es_send.at[h], es_recv.at[h], {"cols": 1 - c})

    def span(piece):
        return pl.ds(0, head) if piece == 0 else pl.ds(head, 16)

    def act_copy(piece, source, d, where):
        part = abuf.at[source + 1, span(piece)]
        return remote(part, part, a_send.at[piece, d], a_recv.at[piece, source], {"rows": where})

    def first_copy(h, plane, d, where):
        part = fbuf.at[h, plane]
        return remote(part, part, f_send.at[h, d], f_recv.at[h, plane], {"rows": where})

    def out_copy(h, plane):
        return remote(osend.at[h], orecv.at[plane], o_send.at[h], o_recv.at[plane], {"rows": h})

    def past_copy(v, h):
        return remote(psend.at[v, h], precv.at[v, h], p_send.at[v, h], p_recv.at[v, h], {"tm": t + 1})

    def outer_column(act):
        cube = act.reshape(frames, width, chans)
        edge = jnp.where(c == 0, cube[:, width - 1, :], cube[:, 0, :])
        edge = jnp.concatenate([edge, jnp.zeros((16 - frames, chans), jnp.float32)], axis=0)
        return edge.astype(jnp.bfloat16)

    def pack(full):
        rows = full[0:keep]
        if tail:
            slices = [full[keep:cells, q * spare : (q + 1) * spare] for q in range(n_out // spare)]
            rest = keep - tail * len(slices)
            if rest:
                slices.append(jnp.zeros((rest, spare), jnp.float32))
            rows = jnp.concatenate([rows[:, 0:n_out], jnp.concatenate(slices, axis=0)], axis=1)
        if packed > keep:
            rows = jnp.concatenate([rows, jnp.zeros((packed - keep, lanes), jnp.float32)], axis=0)
        return rows.astype(jnp.bfloat16)

    def unpack(ref):
        rows = ref[...].astype(jnp.float32)
        main = rows[0:keep, 0:n_out]
        if tail:
            last = [rows[q * tail : (q + 1) * tail, n_out:lanes] for q in range(n_out // spare)]
            main = jnp.concatenate([main, jnp.concatenate(last, axis=1)], axis=0)
        return main

    def prepare(h):
        for d in distances:
            first_copy(h, peer(d), 0, r).wait_recv()
        first_out = jnp.concatenate([unpack(fbuf.at[h, j]) for j in range(n_rows)], axis=1)
        act = activate(first_out, g2_ref[...].reshape(1, chans))
        edges_out[h] = outer_column(act)
        edges_copy(h).start()
        rows = jnp.concatenate([act, jnp.zeros((block - cells, chans), jnp.float32)], axis=0)
        bbuf[h + 1] = rows.astype(jnp.bfloat16)

    def complete(h):
        edges_copy(h).wait_recv()
        rows = bbuf[h + 1, head:block].astype(jnp.float32)
        got = edges_in[h].astype(jnp.float32)
        rows = jnp.concatenate([rows[0 : cells - head], got[0 : block - cells]], axis=0)
        bbuf[h + 1, head:block] = rows.astype(jnp.bfloat16)

    def arrive(h):
        @pl.when(h != r)
        def _():
            for piece in range(2):
                act_copy(piece, h, 0, r).wait_recv()

    def convolve(v):
        bias_all = biases[v][...].reshape(1, chans)
        bias = jnp.zeros((1, n_out), jnp.float32)
        for j in range(n_rows):
            bias = bias + jnp.where(r == j, bias_all[:, j * n_out : (j + 1) * n_out], 0.0)
        if n_out < lanes:
            bias = jnp.concatenate([bias, jnp.zeros((1, lanes - n_out), jnp.float32)], axis=1)
        column = lax.broadcasted_iota(jnp.int32, (width, lanes), 0)
        edge_column = jnp.where(c == 0, width - 1, 0)

        def finish(h):
            @pl.when(has_prev)
            def _():
                past_copy(v, h).wait_recv()

            slot = lax.rem(h, 2)
            rows = obuf[slot, 0:cells]
            past = precv[v, h].astype(jnp.float32)
            rows = jnp.concatenate([rows[0 : 2 * width] + past, rows[2 * width : cells]], axis=0)
            rows = pack(rows + bias)
            if v == 0:
                fbuf[h, r] = rows
                for d in distances:
                    first_copy(h, r, d, peer(d)).start()
            else:
                @pl.when(h == r)
                def _():
                    orecv[r] = rows

                @pl.when(h != r)
                def _():
                    osend[h] = rows
                    out_copy(h, r).start()

        get = arrive if v == 0 else prepare
        get(0)
        for row_tap in range(3):
            weight_copy(v, row_tap).wait()
        if v == 1:
            complete(0)

        def step(h, carry):
            more = h + 1 < n_rows

            @pl.when(more)
            def _():
                get(h + 1)

            @pl.when(h > 0)
            def _():
                finish(h - 1)

            if v == 1:
                @pl.when(more)
                def _():
                    complete(h + 1)

            source = acts[v]
            window = jnp.concatenate([source[h], source[h + 1], source[h + 2]], axis=1)
            kernel_all = wbuf[v].reshape(9 * lanes, 3 * chans)
            zbuf[...] = lax.dot_general(
                window, kernel_all, (((1,), (1,)), ((), ())), preferred_element_type=jnp.float32
            )
            slot = lax.rem(h, 2)

            def piece(f, tap, s):
                at = (3 * tap + s) * lanes
                return zbuf[f * width : (f + 1) * width, at : at + lanes]

            sides = []
            for tap in range(3):
                left = zbuf[cells : cells + 8, 3 * tap * lanes : (3 * tap + 1) * lanes]
                right = zbuf[cells : cells + 8, (3 * tap + 2) * lanes : (3 * tap + 3) * lanes]
                sides.append(jnp.where(c == 0, right, left))
            for g in (*range(frames, frames + 2), *range(frames)):
                taps = [tap for tap in range(3) if 0 <= g - 2 + tap < frames]
                left, mid, right = (
                    functools.reduce(jnp.add, [piece(g - 2 + tap, tap, s) for tap in taps]) for s in range(3)
                )
                side = functools.reduce(
                    jnp.add, [sides[tap][g - 2 + tap : g - 1 + tap, :] for tap in taps]
                )
                total = mid + jnp.where(column > 0, pltpu.roll(left, 1, 0), 0.0)
                total = total + jnp.where(column < width - 1, pltpu.roll(right, width - 1, 0), 0.0)
                total = total + jnp.where(column == edge_column, side, 0.0)
                obuf[slot, g * width : (g + 1) * width, :] = total
                if g == frames + 1:
                    @pl.when(has_next)
                    def _():
                        psend[v, h] = obuf[slot, cells : cells + 2 * width, :].astype(jnp.bfloat16)
                        past_copy(v, h).start()

            return carry

        lax.fori_loop(0, n_rows, step, 0)
        finish(n_rows - 1)

    fetch.wait()
    act = activate(
        x_ref[...].astype(jnp.float32).reshape(cells, chans), g1_ref[...].reshape(1, chans)
    )
    edge_out[...] = outer_column(act)
    pl.semaphore_wait(
        barrier, n_rows + jnp.where(has_next, 1, 0) + jnp.where(has_prev, 1, 0)
    )
    edge_copy().start()
    abuf[r + 1, 0:head] = act[0:head].astype(jnp.bfloat16)
    for d in distances:
        act_copy(0, r, d, peer(d)).start()
    edge_copy().wait_recv()
    got = edge_in[...].astype(jnp.float32)
    last = jnp.concatenate([act[head:cells], got[0 : block - cells]], axis=0)
    abuf[r + 1, head:block] = last.astype(jnp.bfloat16)
    for d in distances:
        act_copy(1, r, d, peer(d)).start()

    convolve(0)
    convolve(1)

    for d in distances:
        j = peer(d)
        out_copy(j, j).wait_recv()
    branch = jnp.concatenate([unpack(orecv.at[j]) for j in range(n_rows)], axis=1)
    latents = x_ref[...].astype(jnp.float32).reshape(cells, chans)
    out_ref[...] = (latents + branch).reshape(frames, 1, width, chans).astype(jnp.bfloat16)

    edge_copy().wait_send()
    for d in distances:
        for piece in range(2):
            act_copy(piece, r, d, peer(d)).wait_send()
        out_copy(peer(d), r).wait_send()

    def drain(h, carry):
        edges_copy(h).wait_send()
        for d in distances:
            first_copy(h, r, d, peer(d)).wait_send()

        @pl.when(has_next)
        def _():
            for v in range(2):
                past_copy(v, h).wait_send()

        return carry

    lax.fori_loop(0, n_rows, drain, 0)


def solution(mesh):
    n_rows = mesh.shape["rows"]
    n_tm = mesh.shape["tm"]

    def shards(latents, gain_one, conv_one, bias_one, gain_two, conv_two, bias_two):
        frames, _, width, chans = latents.shape
        n_out = conv_one.shape[1]
        lanes = up(n_out, 128)
        cells = frames * width
        block = up(cells + frames, 16)
        spare = lanes - n_out
        tail = 0
        if spare and n_out % spare == 0:
            tail = cells // (n_out // spare + 1) // 8 * 8
        packed = up(cells - tail, 16)

        def taps(weight):
            weight = weight.reshape(3, 3, 3, n_out, chans)
            extra = up(n_out, 16) - n_out
            if extra:
                weight = jnp.pad(weight, ((0, 0), (0, 0), (0, 0), (0, extra), (0, 0)))
            return weight

        vmem = pl.BlockSpec(memory_space=pltpu.VMEM)
        hbm = pl.BlockSpec(memory_space=pl.ANY)
        dma = pltpu.SemaphoreType.DMA
        bf16 = jnp.bfloat16
        flops = 2 * 2 * n_rows * frames * width * 27 * chans * n_out
        return pl.pallas_call(
            functools.partial(kernel, n_rows, n_tm, n_out, tail),
            out_shape=jax.ShapeDtypeStruct(latents.shape, bf16),
            in_specs=[hbm, vmem, hbm, vmem, vmem, hbm, vmem],
            out_specs=vmem,
            scratch_shapes=[
                pltpu.VMEM(latents.shape, bf16),
                pltpu.VMEM((n_rows + 2, block, chans), bf16),
                pltpu.VMEM((n_rows + 2, block, chans), bf16),
                pltpu.VMEM((2, 3, 3, lanes, 3 * chans), bf16),
                pltpu.VMEM((block, 9 * lanes), jnp.float32),
                pltpu.VMEM((2, up((frames + 2) * width, 16), lanes), jnp.float32),
                pltpu.VMEM((n_rows, n_rows, packed, lanes), bf16),
                pltpu.VMEM((n_rows, packed, lanes), bf16),
                pltpu.VMEM((n_rows, packed, lanes), bf16),
                pltpu.VMEM((2, n_rows, 2 * width, lanes), bf16),
                pltpu.VMEM((2, n_rows, 2 * width, lanes), bf16),
                pltpu.VMEM((16, chans), bf16),
                pltpu.VMEM((16, chans), bf16),
                pltpu.VMEM((n_rows, 16, chans), bf16),
                pltpu.VMEM((n_rows, 16, chans), bf16),
                dma,
                dma((2, 3)),
                dma((2, n_rows)),
                dma((2, n_rows)),
                dma,
                dma,
                dma((n_rows,)),
                dma((n_rows,)),
                dma((n_rows, n_rows)),
                dma((n_rows, n_rows)),
                dma((n_rows,)),
                dma((n_rows,)),
                dma((2, n_rows)),
                dma((2, n_rows)),
            ],
            compiler_params=pltpu.CompilerParams(
                collective_id=0, has_side_effects=True, vmem_limit_bytes=60 * 1024 * 1024
            ),
            cost_estimate=pl.CostEstimate(flops=flops, bytes_accessed=8 * 1024 * 1024, transcendentals=0),
        )(
            latents,
            gain_one,
            taps(conv_one),
            bias_one,
            gain_two,
            taps(conv_two),
            bias_two,
        )

    return jax.shard_map(
        shards,
        mesh=mesh,
        in_specs=(
            P(("groups", "tm"), "rows", "cols", None),
            P(),
            P(None, "rows", None),
            P(),
            P(),
            P(None, "rows", None),
            P(),
        ),
        out_specs=P(("groups", "tm"), "rows", "cols", None),
        check_vma=False,
    )
```

```python
import functools

import jax
import jax.numpy as jnp
from jax import lax
from jax.experimental import pallas as pl
from jax.experimental.pallas import tpu as pltpu
from jax.sharding import PartitionSpec as P

MESH = pl.DeviceIdType.MESH
EPS = 1e-06


def up(value, multiple):
    return -(-value // multiple) * multiple


def activate(values, gain_values):
    mean_square = jnp.mean(values * values, axis=-1, keepdims=True)
    return jax.nn.silu(values * lax.rsqrt(mean_square + EPS) * gain_values)


def kernel(
    n_rows, n_tm, n_out, tail,
    x_hbm, g1_ref, w1_ref, b1_ref, g2_ref, w2_ref, b2_ref, out_ref, x_ref,
    abuf, bbuf, wbuf, zbuf, obuf, fbuf, osend, orecv, psend, precv,
    edge_out, edge_in, edges_out, edges_in,
    x_sem, w_sem, a_send, a_recv, e_send, e_recv, es_send, es_recv,
    ra_send, rf_send, f_send, f_recv, o_send, o_recv, p_send, p_recv,
):
    frames, _, width, chans = x_ref.shape
    cells = frames * width
    block = abuf.shape[1]
    head = block - 16
    third = up(-(-head // 3), 16)
    pieces = [(at, min(third, head - at)) for at in range(0, head, third)] + [(head, 16)]
    far = len(pieces) - 1
    lanes = wbuf.shape[3]
    packed = fbuf.shape[2]
    keep = cells - tail
    spare = lanes - n_out
    r = lax.axis_index("rows")
    t = lax.axis_index("tm")
    c = lax.axis_index("cols")
    weights = (w1_ref, w2_ref)
    biases = (b1_ref, b2_ref)
    acts = (abuf, bbuf)
    has_next = t + 1 < n_tm
    has_prev = t > 0
    distances = sorted(range(1, n_rows), key=lambda d: min(d, n_rows - d))

    def peer(d):
        return lax.rem(r + d, n_rows)

    def weight_copy(v, row_tap):
        return pltpu.make_async_copy(
            weights[v].at[:, row_tap],
            wbuf.at[v, :, :, pl.ds(0, weights[v].shape[3]), pl.ds(row_tap * chans, chans)],
            w_sem.at[v, row_tap],
        )

    def remote(src, dst, send, recv, where):
        return pltpu.make_async_remote_copy(
            src_ref=src, dst_ref=dst, send_sem=send, recv_sem=recv, device_id=where, device_id_type=MESH
        )

    fetch = pltpu.make_async_copy(x_hbm, x_ref, x_sem)
    fetch.start()
    for v in range(2):
        for row_tap in range(3):
            weight_copy(v, row_tap).start()

    barrier = pltpu.get_barrier_semaphore()

    def greet(where):
        pl.semaphore_signal(barrier, inc=1, device_id=where, device_id_type=MESH)

    for d in distances:
        greet({"rows": peer(d)})
    greet({"cols": 1 - c})

    @pl.when(has_next)
    def _():
        greet({"tm": t + 1})

    @pl.when(has_prev)
    def _():
        greet({"tm": t - 1})

    filled = weights[0].shape[3]
    for v in range(2):
        acts[v][0] = jnp.zeros((block, chans), jnp.bfloat16)
        acts[v][n_rows + 1] = jnp.zeros((block, chans), jnp.bfloat16)
        if filled < lanes:
            wbuf[v, :, :, filled:, :] = jnp.zeros((3, 3, lanes - filled, 3 * chans), jnp.bfloat16)

    @pl.when(t == 0)
    def _():
        precv[...] = jnp.zeros(precv.shape, precv.dtype)

    def edge_copy():
        return remote(edge_out, edge_in, e_send, e_recv, {"cols": 1 - c})

    def edges_copy(h):
        return remote(edges_out.at[h], edges_in.at[h], es_send.at[h], es_recv.at[h], {"cols": 1 - c})

    offsets = (2, -2, 1, -1)

    def inside(j):
        return (j >= 0) & (j < n_rows)

    def relayed(s):
        return ((s <= r - 2) & (r + 1 < n_rows)) | ((s >= r + 2) & (r >= 1))

    def near(action):
        for o in offsets:
            @pl.when(inside(r + o))
            def _(o=o):
                action(o + 2, r + o)

    def relays(action):
        for distance in range(2, n_rows):
            for sign in (1, -1):
                @pl.when(inside(r - sign * distance) & inside(r + sign))
                def _(distance=distance, sign=sign):
                    action(r - sign * distance, r + sign)

    def span(piece):
        return pl.ds(*pieces[piece])

    def act_copy(piece, source, d, where):
        part = abuf.at[source + 1, span(piece)]
        return remote(part, part, a_send.at[piece, d], a_recv.at[piece, source], {"rows": where})

    def act_relay(piece, source, where):
        part = abuf.at[source + 1, span(piece)]
        return remote(part, part, ra_send.at[piece, source], a_recv.at[piece, source], {"rows": where})

    def first_relay(h, plane, where):
        part = fbuf.at[h, plane]
        return remote(part, part, rf_send.at[h, plane], f_recv.at[h, plane], {"rows": where})

    def first_copy(h, plane, d, where):
        part = fbuf.at[h, plane]
        return remote(part, part, f_send.at[h, d], f_recv.at[h, plane], {"rows": where})

    def out_copy(h, plane):
        return remote(osend.at[h], orecv.at[plane], o_send.at[h], o_recv.at[plane], {"rows": h})

    def past_copy(v, h):
        return remote(psend.at[v, h], precv.at[v, h], p_send.at[v, h], p_recv.at[v, h], {"tm": t + 1})

    def outer_column(act):
        cube = act.reshape(frames, width, chans)
        edge = jnp.where(c == 0, cube[:, width - 1, :], cube[:, 0, :])
        edge = jnp.concatenate([edge, jnp.zeros((16 - frames, chans), jnp.float32)], axis=0)
        return edge.astype(jnp.bfloat16)

    def pack(full):
        rows = full[0:keep]
        if tail:
            slices = [full[keep:cells, q * spare : (q + 1) * spare] for q in range(n_out // spare)]
            rest = keep - tail * len(slices)
            if rest:
                slices.append(jnp.zeros((rest, spare), jnp.float32))
            rows = jnp.concatenate([rows[:, 0:n_out], jnp.concatenate(slices, axis=0)], axis=1)
        if packed > keep:
            rows = jnp.concatenate([rows, jnp.zeros((packed - keep, lanes), jnp.float32)], axis=0)
        return rows.astype(jnp.bfloat16)

    def unpack(ref):
        rows = ref[...].astype(jnp.float32)
        main = rows[0:keep, 0:n_out]
        if tail:
            last = [rows[q * tail : (q + 1) * tail, n_out:lanes] for q in range(n_out // spare)]
            main = jnp.concatenate([main, jnp.concatenate(last, axis=1)], axis=0)
        return main

    def prepare(h):
        for j in range(n_rows):
            @pl.when((r != j) & jnp.logical_not(relayed(j)))
            def _(j=j):
                first_copy(h, j, 0, r).wait_recv()
        first_out = jnp.concatenate([unpack(fbuf.at[h, j]) for j in range(n_rows)], axis=1)
        act = activate(first_out, g2_ref[...].reshape(1, chans))
        edges_out[h] = outer_column(act)
        edges_copy(h).start()
        rows = jnp.concatenate([act, jnp.zeros((block - cells, chans), jnp.float32)], axis=0)
        bbuf[h + 1] = rows.astype(jnp.bfloat16)

    def complete(h):
        edges_copy(h).wait_recv()
        rows = bbuf[h + 1, head:block].astype(jnp.float32)
        got = edges_in[h].astype(jnp.float32)
        rows = jnp.concatenate([rows[0 : cells - head], got[0 : block - cells]], axis=0)
        bbuf[h + 1, head:block] = rows.astype(jnp.bfloat16)

    def arrive(h):
        @pl.when((h != r) & jnp.logical_not(relayed(h)))
        def _():
            for piece in range(len(pieces)):
                act_copy(piece, h, 0, r).wait_recv()

    def relay_acts():
        for piece in range(len(pieces)):
            def hand_on(source, where):
                act_copy(piece, source, 0, r).wait_recv()
                act_relay(piece, source, where).start()

            relays(hand_on)

    def relay_first(h):
        def hand_on(source, where):
            first_copy(h, source, 0, r).wait_recv()
            first_relay(h, source, where).start()

        relays(hand_on)

    def convolve(v):
        bias_all = biases[v][...].reshape(1, chans)
        bias = jnp.zeros((1, n_out), jnp.float32)
        for j in range(n_rows):
            bias = bias + jnp.where(r == j, bias_all[:, j * n_out : (j + 1) * n_out], 0.0)
        if n_out < lanes:
            bias = jnp.concatenate([bias, jnp.zeros((1, lanes - n_out), jnp.float32)], axis=1)
        column = lax.broadcasted_iota(jnp.int32, (width, lanes), 0)
        edge_column = jnp.where(c == 0, width - 1, 0)

        def finish(h):
            @pl.when(has_prev)
            def _():
                past_copy(v, h).wait_recv()

            slot = lax.rem(h, 2)
            rows = obuf[slot, 0:cells]
            past = precv[v, h].astype(jnp.float32)
            rows = jnp.concatenate([rows[0 : 2 * width] + past, rows[2 * width : cells]], axis=0)
            rows = pack(rows + bias)
            if v == 0:
                fbuf[h, r] = rows
                near(lambda d, where: first_copy(h, r, d, where).start())
            else:
                @pl.when(h == r)
                def _():
                    orecv[r] = rows

                @pl.when(h != r)
                def _():
                    osend[h] = rows
                    out_copy(h, r).start()

        get = arrive if v == 0 else prepare
        get(0)
        for row_tap in range(3):
            weight_copy(v, row_tap).wait()
        if v == 1:
            complete(0)

        def step(h, carry):
            more = h + 1 < n_rows
            if v == 1:
                @pl.when(h < min(2, n_rows))
                def _():
                    relay_first(n_rows - min(2, n_rows) + h)

            @pl.when(more)
            def _():
                get(h + 1)

            @pl.when(h > 0)
            def _():
                finish(h - 1)

            if v == 0:
                @pl.when(h > 1)
                def _():
                    relay_first(h - 2)

            if v == 1:
                @pl.when(more)
                def _():
                    complete(h + 1)

            source = acts[v]
            window = jnp.concatenate([source[h], source[h + 1], source[h + 2]], axis=1)
            kernel_all = wbuf[v].reshape(9 * lanes, 3 * chans)
            zbuf[...] = lax.dot_general(
                window, kernel_all, (((1,), (1,)), ((), ())), preferred_element_type=jnp.float32
            )
            slot = lax.rem(h, 2)

            def piece(f, tap, s):
                at = (3 * tap + s) * lanes
                return zbuf[f * width : (f + 1) * width, at : at + lanes]

            sides = []
            for tap in range(3):
                left = zbuf[cells : cells + 8, 3 * tap * lanes : (3 * tap + 1) * lanes]
                right = zbuf[cells : cells + 8, (3 * tap + 2) * lanes : (3 * tap + 3) * lanes]
                sides.append(jnp.where(c == 0, right, left))
            for g in (*range(frames, frames + 2), *range(frames)):
                taps = [tap for tap in range(3) if 0 <= g - 2 + tap < frames]
                left, mid, right = (
                    functools.reduce(jnp.add, [piece(g - 2 + tap, tap, s) for tap in taps]) for s in range(3)
                )
                side = functools.reduce(
                    jnp.add, [sides[tap][g - 2 + tap : g - 1 + tap, :] for tap in taps]
                )
                total = mid + jnp.where(column > 0, pltpu.roll(left, 1, 0), 0.0)
                total = total + jnp.where(column < width - 1, pltpu.roll(right, width - 1, 0), 0.0)
                total = total + jnp.where(column == edge_column, side, 0.0)
                obuf[slot, g * width : (g + 1) * width, :] = total
                if g == frames + 1:
                    @pl.when(has_next)
                    def _():
                        psend[v, h] = obuf[slot, cells : cells + 2 * width, :].astype(jnp.bfloat16)
                        past_copy(v, h).start()

            return carry

        lax.fori_loop(0, n_rows, step, 0)
        finish(n_rows - 1)

    fetch.wait()
    act = activate(
        x_ref[...].astype(jnp.float32).reshape(cells, chans), g1_ref[...].reshape(1, chans)
    )
    edge_out[...] = outer_column(act)
    pl.semaphore_wait(
        barrier, n_rows + jnp.where(has_next, 1, 0) + jnp.where(has_prev, 1, 0)
    )
    edge_copy().start()
    abuf[r + 1, 0:head] = act[0:head].astype(jnp.bfloat16)
    for piece in range(far):
        near(lambda d, where: act_copy(piece, r, d, where).start())
    edge_copy().wait_recv()
    got = edge_in[...].astype(jnp.float32)
    last = jnp.concatenate([act[head:cells], got[0 : block - cells]], axis=0)
    abuf[r + 1, head:block] = last.astype(jnp.bfloat16)
    near(lambda d, where: act_copy(far, r, d, where).start())
    relay_acts()

    convolve(0)
    convolve(1)

    for d in distances:
        j = peer(d)
        out_copy(j, j).wait_recv()
    branch = jnp.concatenate([unpack(orecv.at[j]) for j in range(n_rows)], axis=1)
    latents = x_ref[...].astype(jnp.float32).reshape(cells, chans)
    out_ref[...] = (latents + branch).reshape(frames, 1, width, chans).astype(jnp.bfloat16)

    edge_copy().wait_send()
    for piece in range(len(pieces)):
        near(lambda d, where: act_copy(piece, r, d, where).wait_send())
        relays(lambda source, where: act_relay(piece, source, where).wait_send())
    for d in distances:
        out_copy(peer(d), r).wait_send()

    def drain(h, carry):
        edges_copy(h).wait_send()
        near(lambda d, where: first_copy(h, r, d, where).wait_send())
        relays(lambda source, where: first_relay(h, source, where).wait_send())

        @pl.when(has_next)
        def _():
            for v in range(2):
                past_copy(v, h).wait_send()

        return carry

    lax.fori_loop(0, n_rows, drain, 0)


def solution(mesh):
    n_rows = mesh.shape["rows"]
    n_tm = mesh.shape["tm"]

    def shards(latents, gain_one, conv_one, bias_one, gain_two, conv_two, bias_two):
        frames, _, width, chans = latents.shape
        n_out = conv_one.shape[1]
        lanes = up(n_out, 128)
        cells = frames * width
        block = up(cells + frames, 16)
        spare = lanes - n_out
        tail = 0
        if spare and n_out % spare == 0:
            tail = cells // (n_out // spare + 1) // 8 * 8
        packed = up(cells - tail, 16)

        def taps(weight):
            weight = weight.reshape(3, 3, 3, n_out, chans)
            extra = up(n_out, 16) - n_out
            if extra:
                weight = jnp.pad(weight, ((0, 0), (0, 0), (0, 0), (0, extra), (0, 0)))
            return weight

        vmem = pl.BlockSpec(memory_space=pltpu.VMEM)
        hbm = pl.BlockSpec(memory_space=pl.ANY)
        dma = pltpu.SemaphoreType.DMA
        bf16 = jnp.bfloat16
        flops = 2 * 2 * n_rows * frames * width * 27 * chans * n_out
        return pl.pallas_call(
            functools.partial(kernel, n_rows, n_tm, n_out, tail),
            out_shape=jax.ShapeDtypeStruct(latents.shape, bf16),
            in_specs=[hbm, vmem, hbm, vmem, vmem, hbm, vmem],
            out_specs=vmem,
            scratch_shapes=[
                pltpu.VMEM(latents.shape, bf16),
                pltpu.VMEM((n_rows + 2, block, chans), bf16),
                pltpu.VMEM((n_rows + 2, block, chans), bf16),
                pltpu.VMEM((2, 3, 3, lanes, 3 * chans), bf16),
                pltpu.VMEM((block, 9 * lanes), jnp.float32),
                pltpu.VMEM((2, up((frames + 2) * width, 16), lanes), jnp.float32),
                pltpu.VMEM((n_rows, n_rows, packed, lanes), bf16),
                pltpu.VMEM((n_rows, packed, lanes), bf16),
                pltpu.VMEM((n_rows, packed, lanes), bf16),
                pltpu.VMEM((2, n_rows, 2 * width, lanes), bf16),
                pltpu.VMEM((2, n_rows, 2 * width, lanes), bf16),
                pltpu.VMEM((16, chans), bf16),
                pltpu.VMEM((16, chans), bf16),
                pltpu.VMEM((n_rows, 16, chans), bf16),
                pltpu.VMEM((n_rows, 16, chans), bf16),
                dma,
                dma((2, 3)),
                dma((4, 5)),
                dma((4, n_rows)),
                dma,
                dma,
                dma((n_rows,)),
                dma((n_rows,)),
                dma((4, n_rows)),
                dma((n_rows, n_rows)),
                dma((n_rows, 5)),
                dma((n_rows, n_rows)),
                dma((n_rows,)),
                dma((n_rows,)),
                dma((2, n_rows)),
                dma((2, n_rows)),
            ],
            compiler_params=pltpu.CompilerParams(
                collective_id=0, has_side_effects=True, vmem_limit_bytes=60 * 1024 * 1024
            ),
            cost_estimate=pl.CostEstimate(flops=flops, bytes_accessed=8 * 1024 * 1024, transcendentals=0),
        )(
            latents,
            gain_one,
            taps(conv_one),
            bias_one,
            gain_two,
            taps(conv_two),
            bias_two,
        )

    return jax.shard_map(
        shards,
        mesh=mesh,
        in_specs=(
            P(("groups", "tm"), "rows", "cols", None),
            P(),
            P(None, "rows", None),
            P(),
            P(),
            P(None, "rows", None),
            P(),
        ),
        out_specs=P(("groups", "tm"), "rows", "cols", None),
        check_vma=False,
    )
```

```python
import functools

import jax
import jax.numpy as jnp
from jax import lax
from jax.experimental import pallas as pl
from jax.experimental.pallas import tpu as pltpu
from jax.sharding import PartitionSpec as P

MESH = pl.DeviceIdType.MESH
EPS = 1e-06


def up(value, multiple):
    return -(-value // multiple) * multiple


def activate(values, gain_values):
    mean_square = jnp.mean(values * values, axis=-1, keepdims=True)
    return jax.nn.silu(values * lax.rsqrt(mean_square + EPS) * gain_values)


def kernel(
    n_rows, n_tm, n_out, tail,
    x_hbm, g1_ref, w1_ref, b1_ref, g2_ref, w2_ref, b2_ref, out_ref, x_ref,
    abuf, bbuf, wbuf, zbuf, obuf, fbuf, osend, orecv, psend, precv,
    edge_out, edge_in, edges_out, edges_in,
    x_sem, w_sem, a_send, a_recv, e_send, e_recv, es_send, es_recv,
    ra_send, rf_send, f_send, f_recv, o_send, o_recv, p_send, p_recv,
):
    frames, _, width, chans = x_ref.shape
    cells = frames * width
    block = abuf.shape[1]
    head = block - 16
    third = up(-(-head // 3), 16)
    pieces = [(at, min(third, head - at)) for at in range(0, head, third)] + [(head, 16)]
    far = len(pieces) - 1
    lanes = wbuf.shape[3]
    packed = fbuf.shape[2]
    keep = cells - tail
    spare = lanes - n_out
    r = lax.axis_index("rows")
    t = lax.axis_index("tm")
    c = lax.axis_index("cols")
    weights = (w1_ref, w2_ref)
    biases = (b1_ref, b2_ref)
    acts = (abuf, bbuf)
    has_next = t + 1 < n_tm
    has_prev = t > 0
    distances = sorted(range(1, n_rows), key=lambda d: min(d, n_rows - d))

    def peer(d):
        return lax.rem(r + d, n_rows)

    def weight_copy(v, row_tap):
        return pltpu.make_async_copy(
            weights[v].at[:, row_tap],
            wbuf.at[v, :, :, pl.ds(0, weights[v].shape[3]), pl.ds(row_tap * chans, chans)],
            w_sem.at[v, row_tap],
        )

    def remote(src, dst, send, recv, where):
        return pltpu.make_async_remote_copy(
            src_ref=src, dst_ref=dst, send_sem=send, recv_sem=recv, device_id=where, device_id_type=MESH
        )

    fetch = pltpu.make_async_copy(x_hbm, x_ref, x_sem)
    fetch.start()
    for v in range(2):
        for row_tap in range(3):
            weight_copy(v, row_tap).start()

    barrier = pltpu.get_barrier_semaphore()

    def greet(where):
        pl.semaphore_signal(barrier, inc=1, device_id=where, device_id_type=MESH)

    for d in distances:
        greet({"rows": peer(d)})
    greet({"cols": 1 - c})

    @pl.when(has_next)
    def _():
        greet({"tm": t + 1})

    @pl.when(has_prev)
    def _():
        greet({"tm": t - 1})

    filled = weights[0].shape[3]
    for v in range(2):
        acts[v][0] = jnp.zeros((block, chans), jnp.bfloat16)
        acts[v][n_rows + 1] = jnp.zeros((block, chans), jnp.bfloat16)
        if filled < lanes:
            wbuf[v, :, :, filled:, :] = jnp.zeros((3, 3, lanes - filled, 3 * chans), jnp.bfloat16)

    @pl.when(t == 0)
    def _():
        precv[...] = jnp.zeros(precv.shape, precv.dtype)

    def edge_copy():
        return remote(edge_out, edge_in, e_send, e_recv, {"cols": 1 - c})

    def edges_copy(h):
        return remote(edges_out.at[h], edges_in.at[h], es_send.at[h], es_recv.at[h], {"cols": 1 - c})

    offsets = (2, -2, 1, -1)

    def inside(j):
        return (j >= 0) & (j < n_rows)

    def relayed(s):
        return ((s <= r - 2) & (r + 1 < n_rows)) | ((s >= r + 2) & (r >= 1))

    def near(action):
        for o in offsets:
            @pl.when(inside(r + o))
            def _(o=o):
                action(o + 2, r + o)

    def relays(action):
        for distance in range(2, n_rows):
            for sign in (1, -1):
                @pl.when(inside(r - sign * distance) & inside(r + sign))
                def _(distance=distance, sign=sign):
                    action(r - sign * distance, r + sign)

    def span(piece):
        return pl.ds(*pieces[piece])

    def act_copy(piece, source, d, where):
        part = abuf.at[source + 1, span(piece)]
        return remote(part, part, a_send.at[piece, d], a_recv.at[piece, source], {"rows": where})

    def act_relay(piece, source, where):
        part = abuf.at[source + 1, span(piece)]
        return remote(part, part, ra_send.at[piece, source], a_recv.at[piece, source], {"rows": where})

    def first_relay(h, plane, where):
        part = fbuf.at[h, plane]
        return remote(part, part, rf_send.at[h, plane], f_recv.at[h, plane], {"rows": where})

    def first_copy(h, plane, d, where):
        part = fbuf.at[h, plane]
        return remote(part, part, f_send.at[h, d], f_recv.at[h, plane], {"rows": where})

    def out_copy(h, plane):
        return remote(osend.at[h], orecv.at[plane], o_send.at[h], o_recv.at[plane], {"rows": h})

    def past_copy(v, h):
        return remote(psend.at[v, h], precv.at[v, h], p_send.at[v, h], p_recv.at[v, h], {"tm": t + 1})

    def outer_column(act):
        cube = act.reshape(frames, width, chans)
        edge = jnp.where(c == 0, cube[:, width - 1, :], cube[:, 0, :])
        edge = jnp.concatenate([edge, jnp.zeros((16 - frames, chans), jnp.float32)], axis=0)
        return edge.astype(jnp.bfloat16)

    def pack(full):
        rows = full[0:keep]
        if tail:
            slices = [full[keep:cells, q * spare : (q + 1) * spare] for q in range(n_out // spare)]
            rest = keep - tail * len(slices)
            if rest:
                slices.append(jnp.zeros((rest, spare), jnp.float32))
            rows = jnp.concatenate([rows[:, 0:n_out], jnp.concatenate(slices, axis=0)], axis=1)
        if packed > keep:
            rows = jnp.concatenate([rows, jnp.zeros((packed - keep, lanes), jnp.float32)], axis=0)
        return rows.astype(jnp.bfloat16)

    def unpack(ref):
        rows = ref[...].astype(jnp.float32)
        main = rows[0:keep, 0:n_out]
        if tail:
            last = [rows[q * tail : (q + 1) * tail, n_out:lanes] for q in range(n_out // spare)]
            main = jnp.concatenate([main, jnp.concatenate(last, axis=1)], axis=0)
        return main

    def prepare(h):
        for j in range(n_rows):
            @pl.when((r != j) & jnp.logical_not(relayed(j)))
            def _(j=j):
                first_copy(h, j, 0, r).wait_recv()
        first_out = jnp.concatenate([unpack(fbuf.at[h, j]) for j in range(n_rows)], axis=1)
        act = activate(first_out, g2_ref[...].reshape(1, chans))
        edges_out[h] = outer_column(act)
        edges_copy(h).start()
        rows = jnp.concatenate([act, jnp.zeros((block - cells, chans), jnp.float32)], axis=0)
        bbuf[h + 1] = rows.astype(jnp.bfloat16)

    def complete(h):
        edges_copy(h).wait_recv()
        rows = bbuf[h + 1, head:block].astype(jnp.float32)
        got = edges_in[h].astype(jnp.float32)
        rows = jnp.concatenate([rows[0 : cells - head], got[0 : block - cells]], axis=0)
        bbuf[h + 1, head:block] = rows.astype(jnp.bfloat16)

    def arrive(h):
        @pl.when((h != r) & jnp.logical_not(relayed(h)))
        def _():
            for piece in range(len(pieces)):
                act_copy(piece, h, 0, r).wait_recv()

    def relay_acts():
        for piece in range(len(pieces)):
            def hand_on(source, where):
                act_copy(piece, source, 0, r).wait_recv()
                act_relay(piece, source, where).start()

            relays(hand_on)

    def relay_first(h):
        def hand_on(source, where):
            first_copy(h, source, 0, r).wait_recv()
            first_relay(h, source, where).start()

        relays(hand_on)

    def convolve(v):
        bias_all = biases[v][...].reshape(1, chans)
        bias = jnp.zeros((1, n_out), jnp.float32)
        for j in range(n_rows):
            bias = bias + jnp.where(r == j, bias_all[:, j * n_out : (j + 1) * n_out], 0.0)
        if n_out < lanes:
            bias = jnp.concatenate([bias, jnp.zeros((1, lanes - n_out), jnp.float32)], axis=1)
        column = lax.broadcasted_iota(jnp.int32, (width, lanes), 0)
        edge_column = jnp.where(c == 0, width - 1, 0)

        def finish(h):
            @pl.when(has_prev)
            def _():
                past_copy(v, h).wait_recv()

            slot = lax.rem(h, 2)
            rows = obuf[slot, 0:cells]
            past = precv[v, h].astype(jnp.float32)
            rows = jnp.concatenate([rows[0 : 2 * width] + past, rows[2 * width : cells]], axis=0)
            rows = pack(rows + bias)
            if v == 0:
                fbuf[h, r] = rows
                near(lambda d, where: first_copy(h, r, d, where).start())
            else:
                @pl.when(h == r)
                def _():
                    orecv[r] = rows

                @pl.when(h != r)
                def _():
                    osend[h] = rows
                    out_copy(h, r).start()

        get = arrive if v == 0 else prepare
        get(0)
        for row_tap in range(3):
            weight_copy(v, row_tap).wait()
        if v == 1:
            complete(0)

        def step(h, carry):
            more = h + 1 < n_rows
            if v == 1:
                @pl.when(h < min(2, n_rows))
                def _():
                    relay_first(n_rows - min(2, n_rows) + h)

            @pl.when(more)
            def _():
                get(h + 1)

            @pl.when(h > 0)
            def _():
                finish(h - 1)

            if v == 1:
                @pl.when(more)
                def _():
                    complete(h + 1)

            source = acts[v]

            def multiply(first, count):
                window = jnp.concatenate([source[h + first + q] for q in range(count)], axis=1)
                taps = wbuf[v, :, :, :, first * chans : (first + count) * chans]
                zbuf[...] = lax.dot_general(
                    window, taps.reshape(9 * lanes, count * chans), (((1,), (1,)), ((), ())),
                    preferred_element_type=jnp.float32,
                )

            @pl.when(h == 0)
            def _():
                multiply(1, 2)

            @pl.when((h > 0) & more)
            def _():
                multiply(0, 3)

            @pl.when((h > 0) & jnp.logical_not(more))
            def _():
                multiply(0, 2)

            slot = lax.rem(h, 2)

            def piece(f, tap, s):
                at = (3 * tap + s) * lanes
                return zbuf[f * width : (f + 1) * width, at : at + lanes]

            sides = []
            for tap in range(3):
                left = zbuf[cells : cells + 8, 3 * tap * lanes : (3 * tap + 1) * lanes]
                right = zbuf[cells : cells + 8, (3 * tap + 2) * lanes : (3 * tap + 3) * lanes]
                sides.append(jnp.where(c == 0, right, left))
            for g in (*range(frames, frames + 2), *range(frames)):
                taps = [tap for tap in range(3) if 0 <= g - 2 + tap < frames]
                left, mid, right = (
                    functools.reduce(jnp.add, [piece(g - 2 + tap, tap, s) for tap in taps]) for s in range(3)
                )
                side = functools.reduce(
                    jnp.add, [sides[tap][g - 2 + tap : g - 1 + tap, :] for tap in taps]
                )
                total = mid + jnp.where(column > 0, pltpu.roll(left, 1, 0), 0.0)
                total = total + jnp.where(column < width - 1, pltpu.roll(right, width - 1, 0), 0.0)
                total = total + jnp.where(column == edge_column, side, 0.0)
                obuf[slot, g * width : (g + 1) * width, :] = total
                if g == frames + 1:
                    @pl.when(has_next)
                    def _():
                        psend[v, h] = obuf[slot, cells : cells + 2 * width, :].astype(jnp.bfloat16)
                        past_copy(v, h).start()

            if v == 0:
                @pl.when(h > 1)
                def _():
                    relay_first(h - 2)

            return carry

        lax.fori_loop(0, n_rows, step, 0)
        finish(n_rows - 1)

    fetch.wait()
    act = activate(
        x_ref[...].astype(jnp.float32).reshape(cells, chans), g1_ref[...].reshape(1, chans)
    )
    edge_out[...] = outer_column(act)
    pl.semaphore_wait(
        barrier, n_rows + jnp.where(has_next, 1, 0) + jnp.where(has_prev, 1, 0)
    )
    edge_copy().start()
    abuf[r + 1, 0:head] = act[0:head].astype(jnp.bfloat16)
    for piece in range(far):
        near(lambda d, where: act_copy(piece, r, d, where).start())
    edge_copy().wait_recv()
    got = edge_in[...].astype(jnp.float32)
    last = jnp.concatenate([act[head:cells], got[0 : block - cells]], axis=0)
    abuf[r + 1, head:block] = last.astype(jnp.bfloat16)
    near(lambda d, where: act_copy(far, r, d, where).start())
    relay_acts()

    convolve(0)
    convolve(1)

    for d in distances:
        j = peer(d)
        out_copy(j, j).wait_recv()
    branch = jnp.concatenate([unpack(orecv.at[j]) for j in range(n_rows)], axis=1)
    latents = x_ref[...].astype(jnp.float32).reshape(cells, chans)
    out_ref[...] = (latents + branch).reshape(frames, 1, width, chans).astype(jnp.bfloat16)

    edge_copy().wait_send()
    for piece in range(len(pieces)):
        near(lambda d, where: act_copy(piece, r, d, where).wait_send())
        relays(lambda source, where: act_relay(piece, source, where).wait_send())
    for d in distances:
        out_copy(peer(d), r).wait_send()

    def drain(h, carry):
        edges_copy(h).wait_send()
        near(lambda d, where: first_copy(h, r, d, where).wait_send())
        relays(lambda source, where: first_relay(h, source, where).wait_send())

        @pl.when(has_next)
        def _():
            for v in range(2):
                past_copy(v, h).wait_send()

        return carry

    lax.fori_loop(0, n_rows, drain, 0)


def solution(mesh):
    n_rows = mesh.shape["rows"]
    n_tm = mesh.shape["tm"]

    def shards(latents, gain_one, conv_one, bias_one, gain_two, conv_two, bias_two):
        frames, _, width, chans = latents.shape
        n_out = conv_one.shape[1]
        lanes = up(n_out, 128)
        cells = frames * width
        block = up(cells + frames, 16)
        spare = lanes - n_out
        tail = 0
        if spare and n_out % spare == 0:
            tail = cells // (n_out // spare + 1) // 8 * 8
        packed = up(cells - tail, 16)

        def taps(weight):
            weight = weight.reshape(3, 3, 3, n_out, chans)
            extra = up(n_out, 16) - n_out
            if extra:
                weight = jnp.pad(weight, ((0, 0), (0, 0), (0, 0), (0, extra), (0, 0)))
            return weight

        vmem = pl.BlockSpec(memory_space=pltpu.VMEM)
        hbm = pl.BlockSpec(memory_space=pl.ANY)
        dma = pltpu.SemaphoreType.DMA
        bf16 = jnp.bfloat16
        flops = 2 * 2 * n_rows * frames * width * 27 * chans * n_out
        return pl.pallas_call(
            functools.partial(kernel, n_rows, n_tm, n_out, tail),
            out_shape=jax.ShapeDtypeStruct(latents.shape, bf16),
            in_specs=[hbm, vmem, hbm, vmem, vmem, hbm, vmem],
            out_specs=vmem,
            scratch_shapes=[
                pltpu.VMEM(latents.shape, bf16),
                pltpu.VMEM((n_rows + 2, block, chans), bf16),
                pltpu.VMEM((n_rows + 2, block, chans), bf16),
                pltpu.VMEM((2, 3, 3, lanes, 3 * chans), bf16),
                pltpu.VMEM((block, 9 * lanes), jnp.float32),
                pltpu.VMEM((2, up((frames + 2) * width, 16), lanes), jnp.float32),
                pltpu.VMEM((n_rows, n_rows, packed, lanes), bf16),
                pltpu.VMEM((n_rows, packed, lanes), bf16),
                pltpu.VMEM((n_rows, packed, lanes), bf16),
                pltpu.VMEM((2, n_rows, 2 * width, lanes), bf16),
                pltpu.VMEM((2, n_rows, 2 * width, lanes), bf16),
                pltpu.VMEM((16, chans), bf16),
                pltpu.VMEM((16, chans), bf16),
                pltpu.VMEM((n_rows, 16, chans), bf16),
                pltpu.VMEM((n_rows, 16, chans), bf16),
                dma,
                dma((2, 3)),
                dma((4, 5)),
                dma((4, n_rows)),
                dma,
                dma,
                dma((n_rows,)),
                dma((n_rows,)),
                dma((4, n_rows)),
                dma((n_rows, n_rows)),
                dma((n_rows, 5)),
                dma((n_rows, n_rows)),
                dma((n_rows,)),
                dma((n_rows,)),
                dma((2, n_rows)),
                dma((2, n_rows)),
            ],
            compiler_params=pltpu.CompilerParams(
                collective_id=0, has_side_effects=True, vmem_limit_bytes=60 * 1024 * 1024
            ),
            cost_estimate=pl.CostEstimate(flops=flops, bytes_accessed=8 * 1024 * 1024, transcendentals=0),
        )(
            latents,
            gain_one,
            taps(conv_one),
            bias_one,
            gain_two,
            taps(conv_two),
            bias_two,
        )

    return jax.shard_map(
        shards,
        mesh=mesh,
        in_specs=(
            P(("groups", "tm"), "rows", "cols", None),
            P(),
            P(None, "rows", None),
            P(),
            P(),
            P(None, "rows", None),
            P(),
        ),
        out_specs=P(("groups", "tm"), "rows", "cols", None),
        check_vma=False,
    )
```
